512 devices in a mesh: leaf: 8 (over y), row: 8 (over z_hi, x), col: 8 (over z_lo, core).
Axes of the slice: x: 4, y: 8, z: 8 (z_hi: 2, z_lo: 4; z = z_hi * 4 + z_lo), core: 2. Of those that a mesh axis runs over, the one named last changes fastest.
Arguments:
- parent_front: float32 [2, 1, 8192, 8, 1024], P(None, None, ('leaf', 'row'), None, 'col'), as said below
- child_updates: float32 [2, 1, 8192, 4, 1024], P(None, None, ('leaf', 'row'), None, 'col')
- child_map: int32 [2, 32], replicated, may hold values from 0 to 63, as said below
Outputs:
- factored_front: float32 [2, 1, 8192, 8, 1024], P(None, None, ('leaf', 'row'), None, 'col')
The draws below stay inside these ranges and needn't reach their ends.
Inputs may be any that keep to these rules, and one draw needn't show every extreme that they name: For each child c the entries child_map[c, :] are distinct, child_map[c, a] leaves the same remainder modulo 8 as a, and each child's map contains the first and the last parent block of every remainder class. Each row of the parent front's pivot block has a diagonal entry whose magnitude exceeds the norm of the row's other entries in that block; parent_front and child_updates are complex symmetric.
All inputs are finite; a program needn't handle non-finite values.
Results may differ from the reference program's by a relative error of at most 0.0015.
Values may be sent and summed in bfloat16 or wider, within the bound.
No kernel may reach another device: no remote copies, remote signals or barrier semaphores. Data moves between devices by JAX's collectives and lax.ppermute only.
A program may use at most 64 MiB of HBM per device.

```python
import math
import jax
import jax.numpy as jnp
from jax import lax

BLK = 128
RB = 1
RBC = 1
NS_STEPS = 3
NLR = 64
RESIDUES = 8
PB = 64
PBL = 8
CB = 32
CBLC = 4
P_SIZE = 8192
C = 4096
PANEL = 256


def symmetric_pair(key, order, scale):
    keys = jax.random.split(key, 2)
    real_part = jax.random.normal(keys[0], (order, order), jnp.float32)
    imag_part = jax.random.normal(keys[1], (order, order), jnp.float32)
    real_part = (real_part + real_part.T) * (0.7071 * scale)
    imag_part = (imag_part + imag_part.T) * (0.7071 * scale)
    return (real_part, imag_part)


def draw_parent_front(key, part):
    keys = jax.random.split(key, 3)
    real_part, imag_part = symmetric_pair(keys[0], P_SIZE, 1.0)
    strength = 8.0 * math.sqrt(BLK)
    diag_real = strength * jax.random.uniform(keys[1], (P_SIZE,), jnp.float32, 1.0, 2.0)
    diag_imag = strength * jax.random.uniform(keys[2], (P_SIZE,), jnp.float32, 0.1, 0.5)
    identity = jnp.eye(P_SIZE, dtype=jnp.float32)
    real_part = real_part + identity * diag_real[None, :]
    imag_part = imag_part + identity * diag_imag[None, :]
    return jnp.stack([real_part, imag_part]).reshape(2, RB, NLR * BLK, PBL, P_SIZE // PBL)


def draw_child_updates(key, part):
    pieces = []
    for child_index in range(2):
        real_part, imag_part = symmetric_pair(jax.random.fold_in(key, 17 + child_index), C, 0.5)
        pieces.append(jnp.stack([real_part, imag_part]).reshape(2, RBC, NLR // 2 * BLK, CBLC, C // CBLC))
    return jnp.concatenate(pieces, axis=2)


def draw_child_map(key, part):
    per_class = CB // RESIDUES
    span = PB // RESIDUES

    def one_class(subkey):
        middle = jax.random.permutation(subkey, span - 2)[:per_class - 2] + 1
        middle = jnp.sort(middle.astype(jnp.int32))
        return jnp.concatenate([jnp.zeros((1,), jnp.int32), middle, jnp.full((1,), span - 1, jnp.int32)])
    maps = []
    for child_index in range(2):
        keys = jax.random.split(jax.random.fold_in(key, 101 + child_index), RESIDUES)
        values = jax.vmap(one_class)(keys)
        blocks = jnp.arange(RESIDUES, dtype=jnp.int32)[:, None] + RESIDUES * values
        maps.append(blocks.T.reshape(-1))
    return jnp.stack(maps).astype(jnp.int32)


def setup_inputs(seed: int = 0) -> dict:
    splits = jax.random.split(jax.random.key(seed), 4)
    parent_front = draw_parent_front(jax.random.fold_in(splits[3], 71), 0)
    child_updates = draw_child_updates(jax.random.fold_in(splits[3], 71), 0)
    child_map = draw_child_map(jax.random.fold_in(splits[3], 71), 0)
    return dict(parent_front=parent_front, child_updates=child_updates, child_map=child_map)


def complex_product(left, right):
    real_part = jnp.matmul(left[0], right[0], precision=lax.Precision.HIGHEST) - jnp.matmul(left[1], right[1], precision=lax.Precision.HIGHEST)
    imag_part = jnp.matmul(left[0], right[1], precision=lax.Precision.HIGHEST) + jnp.matmul(left[1], right[0], precision=lax.Precision.HIGHEST)
    return jnp.stack([real_part, imag_part])


def transposed_product(left, right):
    real_part = jnp.einsum("rp,cp->rc", left[0], right[0], preferred_element_type=jnp.float32) - jnp.einsum("rp,cp->rc", left[1], right[1], preferred_element_type=jnp.float32)
    imag_part = jnp.einsum("rp,cp->rc", left[0], right[1], preferred_element_type=jnp.float32) + jnp.einsum("rp,cp->rc", left[1], right[0], preferred_element_type=jnp.float32)
    return jnp.stack([real_part, imag_part])


def newton_inverse(pivot_block):
    diag_real = jnp.diagonal(pivot_block[0])
    diag_imag = jnp.diagonal(pivot_block[1])
    denominator = diag_real * diag_real + diag_imag * diag_imag
    current = jnp.stack([jnp.diag(diag_real / denominator), jnp.diag(-diag_imag / denominator)])
    for newton_step in range(NS_STEPS):
        product = complex_product(pivot_block, current)
        current = 2.0 * current - complex_product(current, product)
    return current


def reference(parent_front, child_updates, child_map):
    assembled = parent_front.reshape(2, PB, BLK, PB, BLK)
    halves = child_updates.reshape(2, RBC, 2, (NLR // 2) * BLK, CBLC, C // CBLC)
    for child_index in range(2):
        update = halves[:, :, child_index].reshape(2, CB, BLK, CB, BLK)
        select = (child_map[child_index][:, None] == jnp.arange(PB, dtype=jnp.int32)[None, :]).astype(jnp.float32)
        assembled = assembled + jnp.einsum("ap,zaxby,bq->zpxqy", select, update, select, precision=lax.Precision.HIGHEST)
    matrix = assembled.reshape(2, P_SIZE, P_SIZE)
    pivot_block = matrix[:, :PANEL, :PANEL]
    panel_cols = matrix[:, :, :PANEL]
    inverse = newton_inverse(pivot_block)
    multipliers = complex_product(panel_cols, inverse)
    update_all = transposed_product(multipliers.astype(jnp.bfloat16), panel_cols.astype(jnp.bfloat16))
    schur_part = matrix - update_all
    row_index = jnp.arange(P_SIZE, dtype=jnp.int32)[None, :, None]
    col_index = jnp.arange(P_SIZE, dtype=jnp.int32)[None, None, :]
    placed = jnp.pad(multipliers, ((0, 0), (0, 0), (0, P_SIZE - PANEL)))
    result = jnp.where(row_index < PANEL, matrix, jnp.where(col_index < PANEL, placed, schur_part))
    return result.reshape(parent_front.shape)
```

```python
import jax
import jax.numpy as jnp
from jax import lax
from jax.experimental import pallas as pl
from jax.experimental.pallas import tpu as pltpu
from jax.sharding import PartitionSpec as P

BLK = 128
SLOTS = 8
CHILD_SLOTS = 4
RANKS = 8
SLICE = BLK // RANKS
F32 = jnp.float32
BF16 = jnp.bfloat16
VMEM_LIMIT = 40 * 1024 * 1024


def vmem():
    return pl.BlockSpec(memory_space=pltpu.VMEM)


def smem():
    return pl.BlockSpec(memory_space=pltpu.SMEM)


def params():
    return pltpu.CompilerParams(vmem_limit_bytes=VMEM_LIMIT)


def top_rows_kernel(map_ref, front_ref, child_ref, out_ref, acc_ref):
    leaf, row, col = (lax.axis_index(name) for name in ("leaf", "row", "col"))
    child = leaf // CHILD_SLOTS
    hit = map_ref[child, (leaf % CHILD_SLOTS) * RANKS + row] == row

    @pl.when(leaf == 0)
    def _():
        for z in range(2):
            for j in range(SLOTS):
                acc_ref[j, z] = front_ref[z, pl.ds(j, BLK, stride=SLOTS), :]

    @pl.when(leaf != 0)
    def _():
        acc_ref[...] = jnp.zeros_like(acc_ref)

    @pl.when(hit)
    def _():
        for k in range(CHILD_SLOTS):
            slot = map_ref[child, k * RANKS + col] // RANKS
            for z in range(2):
                acc_ref[slot, z] += child_ref[z, pl.ds(k, BLK, stride=CHILD_SLOTS), :]

    for d in range(SLOTS):
        for z in range(2):
            out_ref[d, z, :BLK, :] = acc_ref[d, z].astype(BF16)
            out_ref[d, z, BLK:, :] = acc_ref[0, z, d * SLICE : (d + 1) * SLICE, :].astype(BF16)


def top_rows(child_map, front, child):
    return pl.pallas_call(
        top_rows_kernel,
        out_shape=jax.ShapeDtypeStruct((SLOTS, 2, BLK + SLICE, BLK), BF16),
        in_specs=[smem(), vmem(), vmem()],
        out_specs=vmem(),
        scratch_shapes=[pltpu.VMEM((SLOTS, 2, BLK, BLK), F32)],
        compiler_params=params(),
        name="top_rows",
    )(child_map, front, child)


def assemble_kernel(map_ref, front_ref, pieces_ref, out_ref, piece_ref, sem):
    leaf, row, col = (lax.axis_index(name) for name in ("leaf", "row", "col"))
    out_ref[...] = front_ref[...]
    for child in range(2):
        for source in range(CHILD_SLOTS):
            @pl.when(map_ref[child, source * RANKS + row] // RANKS == leaf)
            def _():
                copy = pltpu.make_async_copy(
                    pieces_ref.at[child * CHILD_SLOTS + source], piece_ref, sem
                )
                copy.start()
                copy.wait()
                for k in range(CHILD_SLOTS):
                    slot = map_ref[child, k * RANKS + col] // RANKS
                    for z in range(2):
                        where = pl.ds(slot, BLK, stride=SLOTS)
                        out_ref[z, where, :] += piece_ref[z, pl.ds(k, BLK, stride=CHILD_SLOTS), :]


def assemble(child_map, front, pieces):
    return pl.pallas_call(
        assemble_kernel,
        out_shape=jax.ShapeDtypeStruct(front.shape, F32),
        in_specs=[smem(), vmem(), pl.BlockSpec(memory_space=pl.ANY)],
        out_specs=vmem(),
        scratch_shapes=[pltpu.VMEM(pieces.shape[1:], F32), pltpu.SemaphoreType.DMA],
        compiler_params=params(),
        cost_estimate=pl.CostEstimate(flops=1 << 20, bytes_accessed=3 << 20, transcendentals=0),
        name="assemble",
    )(child_map, front, pieces)


def split(x):
    high = x.astype(BF16)
    return high, (x - high.astype(F32)).astype(BF16)


def dot(a, b):
    return jnp.dot(a, b, preferred_element_type=F32)


def product(left, right):
    ls = [split(x) for x in left]
    rs = [split(x) for x in right]

    def real(a, b):
        return dot(a[0], b[0]) + (dot(a[0], b[1]) + dot(a[1], b[0]))

    return (
        real(ls[0], rs[0]) - real(ls[1], rs[1]),
        real(ls[0], rs[1]) + real(ls[1], rs[0]),
    )


def multipliers_kernel(pieces_ref, rows_ref, left_ref, mult_ref, a_ref):
    width = 2 * BLK
    for d in range(RANKS):
        for h in range(2):
            for z in range(2):
                for g in range(2):
                    a_ref[
                        z, h * BLK + d * SLICE : h * BLK + (d + 1) * SLICE, g * BLK : (g + 1) * BLK
                    ] = pieces_ref[d, h, z, g * SLICE : (g + 1) * SLICE, :].astype(F32)
    a_re, a_im = a_ref[0], a_ref[1]
    diagonal = lax.broadcasted_iota(jnp.int32, (width, width), 0) == lax.broadcasted_iota(
        jnp.int32, (width, width), 1
    )
    d_re = jnp.sum(jnp.where(diagonal, a_re, 0.0), axis=1, keepdims=True)
    d_im = jnp.sum(jnp.where(diagonal, a_im, 0.0), axis=1, keepdims=True)
    size = d_re * d_re + d_im * d_im
    x_re, x_im = d_re / size, -d_im / size
    e_re = jnp.where(diagonal, 0.0, -(x_re * a_re - x_im * a_im))
    e_im = jnp.where(diagonal, 0.0, -(x_re * a_im + x_im * a_re))
    e0 = (e_re, e_im)
    e1 = product(e0, e0)
    e2 = product(e1, e1)
    r_re, r_im = rows_ref[0].astype(F32), rows_ref[1].astype(F32)
    t = (x_re * r_re - x_im * r_im, x_re * r_im + x_im * r_re)
    for e in (e0, e1, e2):
        step = product(e, t)
        t = (t[0] + step[0], t[1] + step[1])
    w_re, w_im = t[0].T, t[1].T
    mult_ref[0] = w_re
    mult_ref[1] = w_im
    left_ref[:BLK, :width] = w_re.astype(BF16)
    left_ref[:BLK, width:] = (-w_im).astype(BF16)
    left_ref[BLK:, :width] = w_im.astype(BF16)
    left_ref[BLK:, width:] = w_re.astype(BF16)


def multipliers(pieces, rows):
    width = 2 * BLK
    return pl.pallas_call(
        multipliers_kernel,
        out_shape=(
            jax.ShapeDtypeStruct((width, 2 * width), BF16),
            jax.ShapeDtypeStruct((2, BLK, width), F32),
        ),
        in_specs=[vmem(), vmem()],
        out_specs=(vmem(), vmem()),
        scratch_shapes=[pltpu.VMEM((2, width, width), F32)],
        compiler_params=params(),
        cost_estimate=pl.CostEstimate(flops=3 << 30, bytes_accessed=1 << 20, transcendentals=0),
        name="multipliers",
    )(pieces, rows)


def update_kernel(left_ref, mult_ref, panel_ref, front_ref, out_ref):
    leaf, row, col = (lax.axis_index(name) for name in ("leaf", "row", "col"))
    is_pivot_row = (leaf == 0) & (row < 2)

    @pl.when(is_pivot_row)
    def _():
        out_ref[...] = front_ref[...]

    @pl.when(jnp.logical_not(is_pivot_row))
    def _():
        left = left_ref[...]
        for j in range(SLOTS):
            update = dot(left, panel_ref[j])
            where = pl.ds(j, BLK, stride=SLOTS)
            for z in range(2):
                out_ref[z, where, :] = front_ref[z, where, :] - update[z * BLK : (z + 1) * BLK]
        for g in range(2):
            @pl.when(col == g)
            def _():
                for z in range(2):
                    out_ref[z, pl.ds(0, BLK, stride=SLOTS), :] = mult_ref[z, :, g * BLK : (g + 1) * BLK]


def update(left, mult, panel, front):
    return pl.pallas_call(
        update_kernel,
        out_shape=jax.ShapeDtypeStruct(front.shape, F32),
        in_specs=[vmem()] * 4,
        out_specs=vmem(),
        compiler_params=params(),
        name="update",
    )(left, mult, panel, front)


def exchange(x, axis):
    return lax.all_to_all(x, axis, 0, 0)


def spread(x, axis):
    return exchange(jnp.broadcast_to(x[None], (RANKS,) + x.shape), axis)


def local(parent_front, child_updates, child_map):
    front = parent_front.reshape(2, BLK * SLOTS, BLK)
    child = child_updates.reshape(2, BLK * CHILD_SLOTS, BLK)
    pieces = lax.all_gather(child, "leaf", axis=0, tiled=False)
    parts = exchange(top_rows(child_map, front, child), "leaf")
    top = jnp.sum(parts.astype(F32), axis=0).astype(BF16)
    pivot = spread(top[:, BLK:], "col")
    both = spread(jnp.concatenate([top[:, :BLK], pivot[0], pivot[1]], axis=1), "row")
    own = jnp.concatenate([both[0, :, :BLK], both[1, :, :BLK]], axis=1)
    panel = lax.all_gather(own, "leaf", axis=0, tiled=False)
    swap = [(a * RANKS + b, b * RANKS + a) for a in range(RANKS) for b in range(RANKS)]
    rows = lax.ppermute(own, ("row", "col"), swap)
    pivot_pieces = spread(both[:2, :, BLK:], "leaf")
    left, mult = multipliers(pivot_pieces, rows)
    assembled = assemble(child_map, front, pieces)
    result = update(left, mult, panel.reshape(SLOTS, 4 * BLK, BLK), assembled)
    return result.reshape(parent_front.shape)


def solution(mesh):
    spec = P(None, None, ("leaf", "row"), None, "col")
    return jax.shard_map(
        local, mesh=mesh, in_specs=(spec, spec, P()), out_specs=spec, check_vma=False
    )
```

```python
import jax
import jax.numpy as jnp
from jax import lax
from jax.experimental import pallas as pl
from jax.experimental.pallas import tpu as pltpu
from jax.sharding import PartitionSpec as P

BLK = 128
SLOTS = 8
CHILD_SLOTS = 4
RANKS = 8
SLICE = BLK // RANKS
F32 = jnp.float32
BF16 = jnp.bfloat16
VMEM_LIMIT = 56 * 1024 * 1024


def vmem():
    return pl.BlockSpec(memory_space=pltpu.VMEM)


def smem():
    return pl.BlockSpec(memory_space=pltpu.SMEM)


def hbm():
    return pl.BlockSpec(memory_space=pltpu.HBM)


def params():
    return pltpu.CompilerParams(vmem_limit_bytes=VMEM_LIMIT)


def top_rows_kernel(map_ref, front_hbm, child_hbm, out_ref, acc_ref, front_ref, child_ref, sems):
    leaf, row, col = (lax.axis_index(name) for name in ("leaf", "row", "col"))
    child = leaf // CHILD_SLOTS
    used = row < 2
    hit = used & (map_ref[child, (leaf % CHILD_SLOTS) * RANKS + row] == row)
    first = used & (leaf == 0)
    front_copy = pltpu.make_async_copy(front_hbm, front_ref, sems.at[0])
    child_copy = pltpu.make_async_copy(child_hbm, child_ref, sems.at[1])

    @pl.when(first)
    def _():
        front_copy.start()

    @pl.when(hit)
    def _():
        child_copy.start()

    @pl.when(first)
    def _():
        front_copy.wait()
        for z in range(2):
            for j in range(SLOTS):
                acc_ref[j, z] = front_ref[z, pl.ds(j, BLK, stride=SLOTS), :]

    @pl.when(jnp.logical_not(first))
    def _():
        acc_ref[...] = jnp.zeros_like(acc_ref)

    @pl.when(hit)
    def _():
        child_copy.wait()
        for k in range(CHILD_SLOTS):
            slot = map_ref[child, k * RANKS + col] // RANKS
            for z in range(2):
                acc_ref[slot, z] += child_ref[z, pl.ds(k, BLK, stride=CHILD_SLOTS), :]

    for d in range(SLOTS):
        for z in range(2):
            out_ref[d, z, :BLK, :] = acc_ref[d, z].astype(BF16)
            out_ref[d, z, BLK:, :] = acc_ref[0, z, d * SLICE : (d + 1) * SLICE, :].astype(BF16)


def top_rows(child_map, front, child):
    return pl.pallas_call(
        top_rows_kernel,
        out_shape=jax.ShapeDtypeStruct((SLOTS, 2, BLK + SLICE, BLK), BF16),
        in_specs=[smem(), hbm(), hbm()],
        out_specs=vmem(),
        scratch_shapes=[
            pltpu.VMEM((SLOTS, 2, BLK, BLK), F32),
            pltpu.VMEM(front.shape, F32),
            pltpu.VMEM(child.shape, F32),
            pltpu.SemaphoreType.DMA((2,)),
        ],
        compiler_params=params(),
        name="top_rows",
    )(child_map, front, child)


def assemble_kernel(map_ref, front_ref, pieces_ref, out_ref, piece_ref, sem):
    leaf, row, col = (lax.axis_index(name) for name in ("leaf", "row", "col"))
    out_ref[...] = front_ref[...]
    for child in range(2):
        for source in range(CHILD_SLOTS):
            @pl.when(map_ref[child, source * RANKS + row] // RANKS == leaf)
            def _():
                copy = pltpu.make_async_copy(
                    pieces_ref.at[child * CHILD_SLOTS + source], piece_ref, sem
                )
                copy.start()
                copy.wait()
                for k in range(CHILD_SLOTS):
                    slot = map_ref[child, k * RANKS + col] // RANKS
                    for z in range(2):
                        where = pl.ds(slot, BLK, stride=SLOTS)
                        out_ref[z, where, :] += piece_ref[z, pl.ds(k, BLK, stride=CHILD_SLOTS), :]


def assemble(child_map, front, pieces):
    return pl.pallas_call(
        assemble_kernel,
        out_shape=jax.ShapeDtypeStruct(front.shape, F32),
        in_specs=[smem(), vmem(), hbm()],
        out_specs=vmem(),
        scratch_shapes=[pltpu.VMEM(pieces.shape[1:], F32), pltpu.SemaphoreType.DMA],
        compiler_params=params(),
        cost_estimate=pl.CostEstimate(flops=1 << 20, bytes_accessed=3 << 20, transcendentals=0),
        name="assemble",
    )(child_map, front, pieces)


def split(x):
    high = x.astype(BF16)
    return high, (x - high.astype(F32)).astype(BF16)


def dot(a, b):
    return jnp.dot(a, b, preferred_element_type=F32)


def product(left, right):
    ls = [split(x) for x in left]
    rs = [split(x) for x in right]

    def real(a, b):
        return dot(a[0], b[0]) + (dot(a[0], b[1]) + dot(a[1], b[0]))

    return (
        real(ls[0], rs[0]) - real(ls[1], rs[1]),
        real(ls[0], rs[1]) + real(ls[1], rs[0]),
    )


def multipliers_kernel(pieces_ref, rows_ref, left_ref, mult_ref, a_ref):
    width = 2 * BLK
    for d in range(RANKS):
        for h in range(2):
            for z in range(2):
                for g in range(2):
                    a_ref[
                        z, h * BLK + d * SLICE : h * BLK + (d + 1) * SLICE, g * BLK : (g + 1) * BLK
                    ] = pieces_ref[d, h, z, g * SLICE : (g + 1) * SLICE, :].astype(F32)
    a_re, a_im = a_ref[0], a_ref[1]
    diagonal = lax.broadcasted_iota(jnp.int32, (width, width), 0) == lax.broadcasted_iota(
        jnp.int32, (width, width), 1
    )
    d_re = jnp.sum(jnp.where(diagonal, a_re, 0.0), axis=1, keepdims=True)
    d_im = jnp.sum(jnp.where(diagonal, a_im, 0.0), axis=1, keepdims=True)
    size = d_re * d_re + d_im * d_im
    x_re, x_im = d_re / size, -d_im / size
    e_re = jnp.where(diagonal, 0.0, -(x_re * a_re - x_im * a_im))
    e_im = jnp.where(diagonal, 0.0, -(x_re * a_im + x_im * a_re))
    e0 = (e_re, e_im)
    e1 = product(e0, e0)
    e2 = product(e1, e1)
    r_re, r_im = rows_ref[0].astype(F32), rows_ref[1].astype(F32)
    t = (x_re * r_re - x_im * r_im, x_re * r_im + x_im * r_re)
    for e in (e0, e1, e2):
        step = product(e, t)
        t = (t[0] + step[0], t[1] + step[1])
    w_re, w_im = t[0].T, t[1].T
    mult_ref[0] = w_re
    mult_ref[1] = w_im
    left_ref[:BLK, :width] = w_re.astype(BF16)
    left_ref[:BLK, width:] = (-w_im).astype(BF16)
    left_ref[BLK:, :width] = w_im.astype(BF16)
    left_ref[BLK:, width:] = w_re.astype(BF16)


def multipliers(pieces, rows):
    width = 2 * BLK
    return pl.pallas_call(
        multipliers_kernel,
        out_shape=(
            jax.ShapeDtypeStruct((width, 2 * width), BF16),
            jax.ShapeDtypeStruct((2, BLK, width), F32),
        ),
        in_specs=[vmem(), vmem()],
        out_specs=(vmem(), vmem()),
        scratch_shapes=[pltpu.VMEM((2, width, width), F32)],
        compiler_params=params(),
        cost_estimate=pl.CostEstimate(flops=3 << 30, bytes_accessed=1 << 20, transcendentals=0),
        name="multipliers",
    )(pieces, rows)


def update_kernel(left_ref, mult_ref, panel_ref, front_ref, out_ref):
    leaf, row, col = (lax.axis_index(name) for name in ("leaf", "row", "col"))
    is_pivot_row = (leaf == 0) & (row < 2)

    @pl.when(is_pivot_row)
    def _():
        out_ref[...] = front_ref[...]

    @pl.when(jnp.logical_not(is_pivot_row))
    def _():
        left = left_ref[...]
        for j in range(SLOTS):
            update = dot(left, panel_ref[j])
            where = pl.ds(j, BLK, stride=SLOTS)
            for z in range(2):
                out_ref[z, where, :] = front_ref[z, where, :] - update[z * BLK : (z + 1) * BLK]
        for g in range(2):
            @pl.when(col == g)
            def _():
                for z in range(2):
                    out_ref[z, pl.ds(0, BLK, stride=SLOTS), :] = mult_ref[z, :, g * BLK : (g + 1) * BLK]


def update(left, mult, panel, front):
    return pl.pallas_call(
        update_kernel,
        out_shape=jax.ShapeDtypeStruct(front.shape, F32),
        in_specs=[vmem()] * 4,
        out_specs=vmem(),
        compiler_params=params(),
        name="update",
    )(left, mult, panel, front)


def exchange(x, axis):
    return lax.all_to_all(x, axis, 0, 0)


def spread(x, axis):
    return exchange(jnp.broadcast_to(x[None], (RANKS,) + x.shape), axis)


def local(parent_front, child_updates, child_map):
    front = parent_front.reshape(2, BLK * SLOTS, BLK)
    child = child_updates.reshape(2, BLK * CHILD_SLOTS, BLK)
    pieces = lax.all_gather(child, "leaf", axis=0, tiled=False)
    parts = exchange(top_rows(child_map, front, child), "leaf")
    top = jnp.sum(parts.astype(F32), axis=0).astype(BF16)
    pivot = spread(top[:, BLK:], "col")
    both = spread(jnp.concatenate([top[:, :BLK], pivot[0], pivot[1]], axis=1), "row")
    own = jnp.concatenate([both[0, :, :BLK], both[1, :, :BLK]], axis=1)
    swap = [(a * RANKS + b, b * RANKS + a) for a in range(RANKS) for b in range(RANKS)]
    rows = lax.ppermute(own, ("row", "col"), swap)
    pivot_pieces, own = lax.optimization_barrier((spread(both[:2, :, BLK:], "leaf"), own))
    panel = spread(own, "leaf")
    left, mult = multipliers(pivot_pieces, rows)
    assembled = assemble(child_map, front, pieces)
    result = update(left, mult, panel.reshape(SLOTS, 4 * BLK, BLK), assembled)
    return result.reshape(parent_front.shape)


def solution(mesh):
    spec = P(None, None, ("leaf", "row"), None, "col")
    return jax.shard_map(
        local, mesh=mesh, in_specs=(spec, spec, P()), out_specs=spec, check_vma=False
    )
```

```python
import jax
import jax.numpy as jnp
from jax import lax
from jax.experimental import pallas as pl
from jax.experimental.pallas import tpu as pltpu
from jax.sharding import PartitionSpec as P

BLK = 128
SLOTS = 8
CHILD_SLOTS = 4
RANKS = 8
SLICE = BLK // RANKS
TAG = 16
QUARTERS = 4
QUARTER = BLK // QUARTERS
F32 = jnp.float32
BF16 = jnp.bfloat16
F16 = jnp.float16
TOP = 13.0
LARGE = 56 * 1024 * 1024
SMALL = 24 * 1024 * 1024


def vmem():
    return pl.BlockSpec(memory_space=pltpu.VMEM)


def smem():
    return pl.BlockSpec(memory_space=pltpu.SMEM)


def hbm():
    return pl.BlockSpec(memory_space=pltpu.HBM)


def params(limit):
    return pltpu.CompilerParams(vmem_limit_bytes=limit)


def top_rows_kernel(map_ref, front_hbm, child_hbm, out_ref, acc_ref, front_ref, child_ref, sems):
    leaf, row, col = (lax.axis_index(name) for name in ("leaf", "row", "col"))
    child = leaf // CHILD_SLOTS
    used = row < 2
    hit = used & (map_ref[child, (leaf % CHILD_SLOTS) * RANKS + row] == row)
    first = used & (leaf == 0)
    front_copy = pltpu.make_async_copy(front_hbm, front_ref, sems.at[0])
    child_copy = pltpu.make_async_copy(child_hbm, child_ref, sems.at[1])

    @pl.when(first)
    def _():
        front_copy.start()

    @pl.when(hit)
    def _():
        child_copy.start()

    @pl.when(first)
    def _():
        front_copy.wait()
        for z in range(2):
            for j in range(SLOTS):
                acc_ref[j, z] = front_ref[z, pl.ds(j, BLK, stride=SLOTS), :]

    @pl.when(jnp.logical_not(first))
    def _():
        acc_ref[...] = jnp.zeros_like(acc_ref)

    @pl.when(hit)
    def _():
        child_copy.wait()
        for k in range(CHILD_SLOTS):
            slot = map_ref[child, k * RANKS + col] // RANKS
            for z in range(2):
                acc_ref[slot, z] += child_ref[z, pl.ds(k, BLK, stride=CHILD_SLOTS), :]

    for d in range(SLOTS):
        for z in range(2):
            out_ref[d, z, :BLK, :] = acc_ref[d, z].astype(BF16)
            out_ref[d, z, BLK:, :] = acc_ref[0, z, d * SLICE : (d + 1) * SLICE, :].astype(BF16)


def top_rows(child_map, front, child):
    return pl.pallas_call(
        top_rows_kernel,
        out_shape=jax.ShapeDtypeStruct((SLOTS, 2, BLK + SLICE, BLK), BF16),
        in_specs=[smem(), hbm(), hbm()],
        out_specs=vmem(),
        scratch_shapes=[
            pltpu.VMEM((SLOTS, 2, BLK, BLK), F32),
            pltpu.VMEM(front.shape, F32),
            pltpu.VMEM(child.shape, F32),
            pltpu.SemaphoreType.DMA((2,)),
        ],
        compiler_params=params(LARGE),
        name="top_rows",
    )(child_map, front, child)


def route_kernel(map_ref, real_ref, imag_ref, out_ref):
    leaf, row = lax.axis_index("leaf"), lax.axis_index("row")
    child = leaf // CHILD_SLOTS
    out_ref[...] = jnp.zeros_like(out_ref)
    for k in range(CHILD_SLOTS):
        target = map_ref[child, k * RANKS + row] // RANKS
        for z, part_ref in enumerate((real_ref, imag_ref)):
            out_ref[target, z] = part_ref[pl.ds(k, BLK, stride=CHILD_SLOTS), :].T


def route(child_map, real_part, imag_part):
    return pl.pallas_call(
        route_kernel,
        out_shape=jax.ShapeDtypeStruct((SLOTS, 2, BLK, BLK), F32),
        in_specs=[smem(), vmem(), vmem()],
        out_specs=vmem(),
        compiler_params=params(SMALL),
        cost_estimate=pl.CostEstimate(flops=1 << 20, bytes_accessed=2 << 20, transcendentals=0),
        name="route",
    )(child_map, real_part, imag_part)


def assemble_kernel(map_ref, front_ref, pieces_ref, out_ref):
    col = lax.axis_index("col")
    out_ref[...] = front_ref[...]
    for child in range(2):
        for k in range(CHILD_SLOTS):
            slot = map_ref[child, k * RANKS + col] // RANKS
            where = pl.ds(slot, BLK, stride=SLOTS)
            for z in range(2):
                out_ref[z, where, :] += pieces_ref[child * CHILD_SLOTS + k, z]


def assemble(child_map, front, pieces):
    return pl.pallas_call(
        assemble_kernel,
        out_shape=jax.ShapeDtypeStruct(front.shape, F32),
        in_specs=[smem(), vmem(), vmem()],
        out_specs=vmem(),
        compiler_params=params(SMALL),
        cost_estimate=pl.CostEstimate(flops=1 << 20, bytes_accessed=3 << 20, transcendentals=0),
        name="assemble",
    )(child_map, front, pieces)


def split(x):
    high = x.astype(BF16)
    return high, (x - high.astype(F32)).astype(BF16)


def dot(a, b):
    return jnp.dot(a, b, preferred_element_type=F32)


def product(left, right):
    ls = [split(x) for x in left]
    rs = [split(x) for x in right]

    def real(a, b):
        return dot(a[0], b[0]) + (dot(a[0], b[1]) + dot(a[1], b[0]))

    return (
        real(ls[0], rs[0]) - real(ls[1], rs[1]),
        real(ls[0], rs[1]) + real(ls[1], rs[0]),
    )


def multipliers_kernel(mine_ref, other_ref, same_ref, cross_ref, mult_ref, sent_ref, a_ref):
    width = 2 * BLK
    left_here = lax.axis_index("col") % 2 == 0
    for d in range(RANKS):
        for h in range(2):
            for z in range(2):
                mine = mine_ref[d, z, h * SLICE : (h + 1) * SLICE, :].astype(F32)
                other = other_ref[d, z, h * SLICE : (h + 1) * SLICE, :].astype(F32)
                where = slice(h * BLK + d * SLICE, h * BLK + (d + 1) * SLICE)
                a_ref[z, where, :BLK] = jnp.where(left_here, mine, other)
                a_ref[z, where, BLK:] = jnp.where(left_here, other, mine)
    a_re, a_im = a_ref[0], a_ref[1]
    diagonal = lax.broadcasted_iota(jnp.int32, (width, width), 0) == lax.broadcasted_iota(
        jnp.int32, (width, width), 1
    )
    d_re = jnp.sum(jnp.where(diagonal, a_re, 0.0), axis=1, keepdims=True)
    d_im = jnp.sum(jnp.where(diagonal, a_im, 0.0), axis=1, keepdims=True)
    size = d_re * d_re + d_im * d_im
    x_re, x_im = d_re / size, -d_im / size
    e_re = jnp.where(diagonal, 0.0, -(x_re * a_re - x_im * a_im))
    e_im = jnp.where(diagonal, 0.0, -(x_re * a_im + x_im * a_re))
    e0 = (e_re, e_im)
    e1 = product(e0, e0)
    e2 = product(e1, e1)
    r_re, r_im = (
        jnp.concatenate(
            [
                jnp.where(left_here, same_ref[z], cross_ref[z]),
                jnp.where(left_here, cross_ref[z], same_ref[z]),
            ],
            axis=0,
        ).astype(F32)
        for z in range(2)
    )
    t = (x_re * r_re - x_im * r_im, x_re * r_im + x_im * r_re)
    for e in (e0, e1, e2):
        step = product(e, t)
        t = (t[0] + step[0], t[1] + step[1])
    w_re, w_im = t[0].T, t[1].T
    mult_ref[0] = w_re
    mult_ref[1] = w_im
    sent_ref[0] = w_re.astype(BF16)
    sent_ref[1] = w_im.astype(BF16)


def multipliers(mine, other, same, cross):
    width = 2 * BLK
    return pl.pallas_call(
        multipliers_kernel,
        out_shape=(
            jax.ShapeDtypeStruct((2, BLK, width), F32),
            jax.ShapeDtypeStruct((2, BLK, width), BF16),
        ),
        in_specs=[vmem()] * 4,
        out_specs=(vmem(), vmem()),
        scratch_shapes=[pltpu.VMEM((2, width, width), F32)],
        compiler_params=params(SMALL),
        cost_estimate=pl.CostEstimate(flops=3 << 30, bytes_accessed=1 << 20, transcendentals=0),
        name="multipliers",
    )(mine, other, same, cross)


def update_kernel(
    w_ref, near_ref, far_ref, mult_ref, front_ref, q0_ref, q1_ref, q2_ref, q3_ref, out_ref, panel_ref
):
    leaf, row, col = (lax.axis_index(name) for name in ("leaf", "row", "col"))
    is_pivot_row = (leaf == 0) & (row < 2)

    @pl.when(is_pivot_row)
    def _():
        out_ref[...] = front_ref[...]

    @pl.when(jnp.logical_not(is_pivot_row))
    def _():
        w_re, w_im = (
            jnp.where(col < 2, w_ref[z], jnp.where(col < 4, near_ref[z], far_ref[z])) for z in range(2)
        )
        left = jnp.concatenate(
            [jnp.concatenate([w_re, -w_im], axis=1), jnp.concatenate([w_im, w_re], axis=1)], axis=0
        )
        for step, part_ref in enumerate((q0_ref, q1_ref, q2_ref, q3_ref)):
            start = ((row % QUARTERS) ^ step) * QUARTER
            for z in range(2):
                for h in range(2):
                    where = pl.ds(pl.multiple_of((z * 2 + h) * BLK + start, QUARTER), QUARTER)
                    panel_ref[:, where, :] = part_ref[:, z, h * QUARTER : (h + 1) * QUARTER]
        for j in range(SLOTS):
            update = dot(left, panel_ref[j])
            where = pl.ds(j, BLK, stride=SLOTS)
            for z in range(2):
                out_ref[z, where, :] = front_ref[z, where, :] - update[z * BLK : (z + 1) * BLK]
        for g in range(2):
            @pl.when(col == g)
            def _():
                for z in range(2):
                    out_ref[z, pl.ds(0, BLK, stride=SLOTS), :] = mult_ref[z, :, g * BLK : (g + 1) * BLK]


def update(w, near, far, mult, front, quarters):
    return pl.pallas_call(
        update_kernel,
        out_shape=jax.ShapeDtypeStruct(front.shape, F32),
        in_specs=[vmem()] * 9,
        out_specs=vmem(),
        scratch_shapes=[pltpu.VMEM((SLOTS, 4 * BLK, BLK), BF16)],
        compiler_params=params(SMALL),
        name="update",
    )(w, near, far, mult, front, *quarters)


def exchange(x, axis):
    return lax.all_to_all(x, axis, 0, 0)


def spread(x, axis):
    return exchange(jnp.broadcast_to(x[None], (RANKS,) + x.shape), axis)


def shrink(child):
    largest = jnp.max(jnp.abs(child))
    exponent = jnp.clip(jnp.floor(jnp.log2(largest)), -100.0, 127.0)
    values = (child * jnp.exp2(TOP - exponent)).astype(F16)
    tag = jnp.broadcast_to(exponent.astype(F16), (TAG, BLK))
    return jnp.concatenate([values[0], tag], axis=0), values[1]


def local(parent_front, child_updates, child_map):
    front = parent_front.reshape(2, BLK * SLOTS, BLK)
    child = child_updates.reshape(2, BLK * CHILD_SLOTS, BLK)
    swap = [(a * RANKS + b, b * RANKS + a) for a in range(RANKS) for b in range(RANKS)]
    real_part, imag_part = shrink(child)
    real_part = lax.ppermute(real_part, ("row", "col"), swap)
    parts = exchange(top_rows(child_map, front, child), "leaf")
    top = jnp.sum(parts.astype(F32), axis=0).astype(BF16)
    top, real_part = lax.optimization_barrier((top, real_part))
    half, pivot = top[:, :BLK], top[:, BLK:]
    parts = half.reshape(2, QUARTERS, QUARTER, BLK).transpose(1, 0, 2, 3)
    parts = jnp.concatenate(
        [
            jnp.concatenate([parts, parts], axis=0),
            jnp.broadcast_to(pivot[None], (RANKS,) + pivot.shape),
        ],
        axis=2,
    )
    both = exchange(parts, "row")
    same = lax.ppermute(
        half, ("row", "col"), [(h * RANKS + b, b * RANKS + h) for h in range(2) for b in range(RANKS)]
    )
    cross = lax.ppermute(
        half,
        ("row", "col"),
        [(h * RANKS + b, b * RANKS + 1 - h) for h in range(2) for b in range(RANKS)],
    )
    both, same, cross = lax.optimization_barrier((both, same, cross))
    imag_part = lax.ppermute(imag_part, ("row", "col"), swap)
    got = spread(
        jnp.concatenate(
            [both[0, :, :QUARTER], both[1, :, :QUARTER], both[0, :, QUARTER:], both[1, :, QUARTER:]],
            axis=1,
        ),
        "leaf",
    )
    body, tag = real_part[: SLOTS * BLK // 2], real_part[SLOTS * BLK // 2 :]
    routed = route(child_map, body.astype(F32), imag_part.astype(F32))
    routed = jnp.concatenate(
        [
            routed.reshape(SLOTS, 2 * BLK, BLK).astype(F16),
            jnp.broadcast_to(tag[None], (SLOTS,) + tag.shape),
        ],
        axis=1,
    )
    _, routed = lax.optimization_barrier((got, routed))
    pieces = exchange(routed, "leaf")
    mine = got[:, :, 2 * QUARTER :]
    other = lax.ppermute(mine, "col", [(0, 1), (1, 0)])
    mult, w = multipliers(mine, other, same, cross)
    quarters = [got[:, :, : 2 * QUARTER]]
    for bit in (1, 2, 3):
        step = [(a, a ^ bit) for a in range(RANKS)]
        quarters.append(lax.ppermute(quarters[0], "row", step))
    col = lax.axis_index("col")
    near = lax.ppermute(w, "col", [(0, 2), (1, 3)])
    far = lax.ppermute(
        jnp.where(col < 2, w, near), "col", [(0, 4), (1, 5), (2, 6), (3, 7)]
    )
    scale = jnp.exp2(pieces[:, 2 * BLK, 0].astype(F32) - TOP)
    pieces = pieces[:, : 2 * BLK].astype(F32) * scale[:, None, None]
    assembled = assemble(child_map, front, pieces.reshape(SLOTS, 2, BLK, BLK))
    result = update(w, near, far, mult, assembled, quarters)
    return result.reshape(parent_front.shape)


def solution(mesh):
    spec = P(None, None, ("leaf", "row"), None, "col")
    return jax.shard_map(
        local, mesh=mesh, in_specs=(spec, spec, P()), out_specs=spec, check_vma=False
    )
```

```python
import jax
import jax.numpy as jnp
from jax import lax
from jax.experimental import pallas as pl
from jax.experimental.pallas import tpu as pltpu
from jax.sharding import PartitionSpec as P

BLK = 128
SLOTS = 8
CHILD_SLOTS = 4
RANKS = 8
SLICE = BLK // RANKS
TAG = 16
QUARTERS = 4
QUARTER = BLK // QUARTERS
F32 = jnp.float32
BF16 = jnp.bfloat16
F16 = jnp.float16
TOP = 13.0
LARGE = 56 * 1024 * 1024
SMALL = 24 * 1024 * 1024


def vmem():
    return pl.BlockSpec(memory_space=pltpu.VMEM)


def smem():
    return pl.BlockSpec(memory_space=pltpu.SMEM)


def hbm():
    return pl.BlockSpec(memory_space=pltpu.HBM)


def params(limit):
    return pltpu.CompilerParams(vmem_limit_bytes=limit)


def top_rows_kernel(map_ref, front_hbm, child_hbm, out_ref, acc_ref, front_ref, child_ref, sems):
    leaf, row, col = (lax.axis_index(name) for name in ("leaf", "row", "col"))
    child = leaf // CHILD_SLOTS
    target = map_ref[child, (leaf % CHILD_SLOTS) * RANKS + row]
    upright = (row >= 2) & (col < 2)
    hit = (row < 2) & (target == row)
    first = (row < 2) & (leaf == 0)
    front_copy = pltpu.make_async_copy(front_hbm, front_ref, sems.at[0])
    child_copy = pltpu.make_async_copy(child_hbm, child_ref, sems.at[1])

    @pl.when(first | upright)
    def _():
        front_copy.start()

    @pl.when(hit | upright)
    def _():
        child_copy.start()

    @pl.when(jnp.logical_not(first))
    def _():
        acc_ref[...] = jnp.zeros_like(acc_ref)

    @pl.when(first)
    def _():
        front_copy.wait()
        for z in range(2):
            for j in range(SLOTS):
                acc_ref[j, z] = front_ref[z, pl.ds(j, BLK, stride=SLOTS), :]

    @pl.when(hit)
    def _():
        child_copy.wait()
        for k in range(CHILD_SLOTS):
            slot = map_ref[child, k * RANKS + col] // RANKS
            for z in range(2):
                acc_ref[slot, z] += child_ref[z, pl.ds(k, BLK, stride=CHILD_SLOTS), :]

    @pl.when(upright)
    def _():
        front_copy.wait()
        child_copy.wait()
        for z in range(2):
            acc_ref[leaf, z] = front_ref[z, pl.ds(0, BLK, stride=SLOTS), :].T
        for k in range(CHILD_SLOTS):
            @pl.when(map_ref[child, k * RANKS + col] < RANKS)
            def _():
                for z in range(2):
                    acc_ref[target // RANKS, z] += child_ref[z, pl.ds(k, BLK, stride=CHILD_SLOTS), :].T

    for d in range(SLOTS):
        for z in range(2):
            out_ref[d, z, :BLK, :] = acc_ref[d, z].astype(BF16)
            out_ref[d, z, BLK:, :] = acc_ref[0, z, d * SLICE : (d + 1) * SLICE, :].astype(BF16)


def top_rows(child_map, front, child):
    return pl.pallas_call(
        top_rows_kernel,
        out_shape=jax.ShapeDtypeStruct((SLOTS, 2, BLK + SLICE, BLK), BF16),
        in_specs=[smem(), hbm(), hbm()],
        out_specs=vmem(),
        scratch_shapes=[
            pltpu.VMEM((SLOTS, 2, BLK, BLK), F32),
            pltpu.VMEM(front.shape, F32),
            pltpu.VMEM(child.shape, F32),
            pltpu.SemaphoreType.DMA((2,)),
        ],
        compiler_params=params(LARGE),
        name="top_rows",
    )(child_map, front, child)


def route_kernel(map_ref, real_ref, upper_ref, lower_ref, out_ref):
    leaf, row = lax.axis_index("leaf"), lax.axis_index("row")
    child = leaf // CHILD_SLOTS
    out_ref[...] = jnp.zeros_like(out_ref)
    for k in range(CHILD_SLOTS):
        target = map_ref[child, k * RANKS + row] // RANKS
        out_ref[target, :BLK, :] = real_ref[pl.ds(k, BLK, stride=CHILD_SLOTS), :].T
        where = pl.ds(k, BLK // 2, stride=CHILD_SLOTS)
        imag = jnp.concatenate([upper_ref[where, :], lower_ref[where, :]], axis=0)
        out_ref[target, BLK : 2 * BLK, :] = imag.T
    for d in range(SLOTS):
        out_ref[d, 2 * BLK :, :] = real_ref[CHILD_SLOTS * BLK :, :]


def route(child_map, real, upper, lower):
    return pl.pallas_call(
        route_kernel,
        out_shape=jax.ShapeDtypeStruct((SLOTS, 2 * BLK + TAG, BLK), F32),
        in_specs=[smem(), vmem(), vmem(), vmem()],
        out_specs=vmem(),
        compiler_params=params(SMALL),
        cost_estimate=pl.CostEstimate(flops=1 << 20, bytes_accessed=2 << 20, transcendentals=0),
        name="route",
    )(child_map, real, upper, lower)


def assemble_kernel(map_ref, front_ref, pieces_ref, out_ref):
    col = lax.axis_index("col")
    out_ref[...] = front_ref[...]
    for child in range(2):
        for k in range(CHILD_SLOTS):
            slot = map_ref[child, k * RANKS + col] // RANKS
            where = pl.ds(slot, BLK, stride=SLOTS)
            for z in range(2):
                out_ref[z, where, :] += pieces_ref[child * CHILD_SLOTS + k, z]


def assemble(child_map, front, pieces):
    return pl.pallas_call(
        assemble_kernel,
        out_shape=jax.ShapeDtypeStruct(front.shape, F32),
        in_specs=[smem(), vmem(), vmem()],
        out_specs=vmem(),
        compiler_params=params(SMALL),
        cost_estimate=pl.CostEstimate(flops=1 << 20, bytes_accessed=3 << 20, transcendentals=0),
        name="assemble",
    )(child_map, front, pieces)


def split(x):
    high = x.astype(BF16)
    return high, (x - high.astype(F32)).astype(BF16)


def dot(a, b):
    return jnp.dot(a, b, preferred_element_type=F32)


def real_product(a, b):
    return dot(a[0], b[0]) if len(a) == 1 else dot(a[0], b[0]) + (dot(a[0], b[1]) + dot(a[1], b[0]))


def product(left, right):
    return (
        real_product(left[0], right[0]) - real_product(left[1], right[1]),
        real_product(left[0], right[1]) + real_product(left[1], right[0]),
    )


def rounded(pair):
    return [(x.astype(BF16),) for x in pair]


def multipliers_kernel(mine_ref, other_ref, half_ref, rest_ref, mult_ref, sent_ref, a_ref):
    width = 2 * BLK
    left_here = lax.axis_index("col") % 2 == 0
    for d in range(RANKS):
        for h in range(2):
            for z in range(2):
                mine = mine_ref[d, z, h * SLICE : (h + 1) * SLICE, :].astype(F32)
                other = other_ref[d, z, h * SLICE : (h + 1) * SLICE, :].astype(F32)
                where = slice(h * BLK + d * SLICE, h * BLK + (d + 1) * SLICE)
                a_ref[z, where, :BLK] = jnp.where(left_here, mine, other)
                a_ref[z, where, BLK:] = jnp.where(left_here, other, mine)
    a_re, a_im = a_ref[0], a_ref[1]
    diagonal = lax.broadcasted_iota(jnp.int32, (width, width), 0) == lax.broadcasted_iota(
        jnp.int32, (width, width), 1
    )
    d_re = jnp.sum(jnp.where(diagonal, a_re, 0.0), axis=1, keepdims=True)
    d_im = jnp.sum(jnp.where(diagonal, a_im, 0.0), axis=1, keepdims=True)
    size = d_re * d_re + d_im * d_im
    x_re, x_im = d_re / size, -d_im / size
    e_re = jnp.where(diagonal, 0.0, -(x_re * a_re - x_im * a_im))
    e_im = jnp.where(diagonal, 0.0, -(x_re * a_im + x_im * a_re))
    e0 = (e_re, e_im)
    e0_high = rounded(e0)
    e1 = rounded(product(e0_high, e0_high))
    e2 = rounded(product(e1, e1))
    r_re, r_im = (
        jnp.concatenate(
            [
                jnp.where(left_here, half_ref[z], rest_ref[z]),
                jnp.where(left_here, rest_ref[z], half_ref[z]),
            ],
            axis=0,
        ).astype(F32)
        for z in range(2)
    )
    t = (x_re * r_re - x_im * r_im, x_re * r_im + x_im * r_re)
    step = product([split(x) for x in e0], [split(x) for x in t])
    t = (t[0] + step[0], t[1] + step[1])
    for e in (e1, e2):
        step = product(e, rounded(t))
        t = (t[0] + step[0], t[1] + step[1])
    w_re, w_im = t[0].T, t[1].T
    mult_ref[0] = w_re
    mult_ref[1] = w_im
    sent_ref[0] = w_re.astype(BF16)
    sent_ref[1] = w_im.astype(BF16)


def multipliers(mine, other, half, rest):
    width = 2 * BLK
    return pl.pallas_call(
        multipliers_kernel,
        out_shape=(
            jax.ShapeDtypeStruct((2, BLK, width), F32),
            jax.ShapeDtypeStruct((2, BLK, width), BF16),
        ),
        in_specs=[vmem()] * 4,
        out_specs=(vmem(), vmem()),
        scratch_shapes=[pltpu.VMEM((2, width, width), F32)],
        compiler_params=params(SMALL),
        cost_estimate=pl.CostEstimate(flops=3 << 30, bytes_accessed=1 << 20, transcendentals=0),
        name="multipliers",
    )(mine, other, half, rest)


def update_kernel(
    w_ref, near_ref, far_ref, mult_ref, front_ref, q0_ref, q1_ref, q2_ref, q3_ref, out_ref, panel_ref
):
    leaf, row, col = (lax.axis_index(name) for name in ("leaf", "row", "col"))
    is_pivot_row = (leaf == 0) & (row < 2)

    @pl.when(is_pivot_row)
    def _():
        out_ref[...] = front_ref[...]

    @pl.when(jnp.logical_not(is_pivot_row))
    def _():
        w_re, w_im = (
            jnp.where(col < 2, w_ref[z], jnp.where(col < 4, near_ref[z], far_ref[z])) for z in range(2)
        )
        left = jnp.concatenate(
            [jnp.concatenate([w_re, -w_im], axis=1), jnp.concatenate([w_im, w_re], axis=1)], axis=0
        )
        for step, part_ref in enumerate((q0_ref, q1_ref, q2_ref, q3_ref)):
            start = ((row % QUARTERS) ^ step) * QUARTER
            for z in range(2):
                for h in range(2):
                    where = pl.ds(pl.multiple_of((z * 2 + h) * BLK + start, QUARTER), QUARTER)
                    panel_ref[:, where, :] = part_ref[:, z, h * QUARTER : (h + 1) * QUARTER]
        for j in range(SLOTS):
            update = dot(left, panel_ref[j])
            where = pl.ds(j, BLK, stride=SLOTS)
            for z in range(2):
                out_ref[z, where, :] = front_ref[z, where, :] - update[z * BLK : (z + 1) * BLK]
        for g in range(2):
            @pl.when(col == g)
            def _():
                for z in range(2):
                    out_ref[z, pl.ds(0, BLK, stride=SLOTS), :] = mult_ref[z, :, g * BLK : (g + 1) * BLK]


def update(w, near, far, mult, front, quarters):
    return pl.pallas_call(
        update_kernel,
        out_shape=jax.ShapeDtypeStruct(front.shape, F32),
        in_specs=[vmem()] * 9,
        out_specs=vmem(),
        scratch_shapes=[pltpu.VMEM((SLOTS, 4 * BLK, BLK), BF16)],
        compiler_params=params(SMALL),
        name="update",
    )(w, near, far, mult, front, *quarters)


def exchange(x, axis):
    return lax.all_to_all(x, axis, 0, 0)


def spread(x, axis):
    return exchange(jnp.broadcast_to(x[None], (RANKS,) + x.shape), axis)


def shrink(child):
    largest = jnp.max(jnp.abs(child))
    exponent = jnp.clip(jnp.floor(jnp.log2(largest)), -100.0, 127.0)
    values = (child * jnp.exp2(TOP - exponent)).astype(F16)
    tag = jnp.broadcast_to(exponent.astype(F16), (TAG, BLK))
    return jnp.concatenate([values[0], tag], axis=0), values[1]


def local(parent_front, child_updates, child_map):
    front = parent_front.reshape(2, BLK * SLOTS, BLK)
    child = child_updates.reshape(2, BLK * CHILD_SLOTS, BLK)
    swap = [(a * RANKS + b, b * RANKS + a) for a in range(RANKS) for b in range(RANKS)]
    real_part, imag_part = shrink(child)
    real_part = lax.ppermute(real_part, ("row", "col"), swap)
    parts = exchange(top_rows(child_map, front, child), "leaf")
    top = jnp.sum(parts.astype(F32), axis=0).astype(BF16)
    top, real_part = lax.optimization_barrier((top, real_part))
    half, pivot = top[:, :BLK], top[:, BLK:]
    parts = half.reshape(2, QUARTERS, QUARTER, BLK).transpose(1, 0, 2, 3)
    parts = jnp.concatenate(
        [
            jnp.concatenate([parts, parts], axis=0),
            jnp.broadcast_to(pivot[None], (RANKS,) + pivot.shape),
        ],
        axis=2,
    )
    both = exchange(parts, "row")
    row, col = lax.axis_index("row"), lax.axis_index("col")
    corner = lax.ppermute(half, ("row", "col"), [(1, RANKS), (RANKS, 1)])
    half = jnp.where((row < 2) & (row != col), corner, half)
    rest = lax.ppermute(half, "col", [(0, 1), (1, 0)])
    upper, lower = imag_part[: CHILD_SLOTS * BLK // 2], imag_part[CHILD_SLOTS * BLK // 2 :]
    upper = lax.ppermute(upper, ("row", "col"), swap)
    both, rest, upper = lax.optimization_barrier((both, rest, upper))
    lower = lax.ppermute(lower, ("row", "col"), swap)
    got = spread(
        jnp.concatenate(
            [both[0, :, :QUARTER], both[1, :, :QUARTER], both[0, :, QUARTER:], both[1, :, QUARTER:]],
            axis=1,
        ),
        "leaf",
    )
    routed = route(child_map, real_part.astype(F32), upper.astype(F32), lower.astype(F32)).astype(F16)
    _, routed = lax.optimization_barrier((got, routed))
    pieces = exchange(routed, "leaf")
    mine = got[:, :, 2 * QUARTER :]
    other = lax.ppermute(mine, "col", [(0, 1), (1, 0)])
    mult, w = multipliers(mine, other, half, rest)
    quarters = [got[:, :, : 2 * QUARTER]]
    for bit in (1, 2, 3):
        step = [(a, a ^ bit) for a in range(RANKS)]
        quarters.append(lax.ppermute(quarters[0], "row", step))
    near = lax.ppermute(w, "col", [(0, 2), (1, 3)])
    far = lax.ppermute(
        jnp.where(col < 2, w, near), "col", [(0, 4), (1, 5), (2, 6), (3, 7)]
    )
    scale = jnp.exp2(pieces[:, 2 * BLK, 0].astype(F32) - TOP)
    pieces = pieces[:, : 2 * BLK].astype(F32) * scale[:, None, None]
    assembled = assemble(child_map, front, pieces.reshape(SLOTS, 2, BLK, BLK))
    result = update(w, near, far, mult, assembled, quarters)
    return result.reshape(parent_front.shape)


def solution(mesh):
    spec = P(None, None, ("leaf", "row"), None, "col")
    return jax.shard_map(
        local, mesh=mesh, in_specs=(spec, spec, P()), out_specs=spec, check_vma=False
    )
```

```python
import jax
import jax.numpy as jnp
from jax import lax
from jax.experimental import pallas as pl
from jax.experimental.pallas import tpu as pltpu
from jax.sharding import PartitionSpec as P

BLK = 128
SLOTS = 8
CHILD_SLOTS = 4
RANKS = 8
SLICE = BLK // RANKS
TAG = 16
QUARTERS = 4
QUARTER = BLK // QUARTERS
F32 = jnp.float32
BF16 = jnp.bfloat16
F16 = jnp.float16
TOP = 13.0
LARGE = 56 * 1024 * 1024
SMALL = 24 * 1024 * 1024


def vmem():
    return pl.BlockSpec(memory_space=pltpu.VMEM)


def smem():
    return pl.BlockSpec(memory_space=pltpu.SMEM)


def hbm():
    return pl.BlockSpec(memory_space=pltpu.HBM)


def params(limit):
    return pltpu.CompilerParams(vmem_limit_bytes=limit)


def top_rows_kernel(map_ref, front_hbm, child_hbm, out_ref, acc_ref, front_ref, child_ref, sems):
    leaf, row, col = (lax.axis_index(name) for name in ("leaf", "row", "col"))
    child = leaf // CHILD_SLOTS
    target = map_ref[child, (leaf % CHILD_SLOTS) * RANKS + row]
    upright = (row >= 2) & (col < 2)
    hit = (row < 2) & (target == row)
    first = (row < 2) & (leaf == 0)
    front_copy = pltpu.make_async_copy(front_hbm, front_ref, sems.at[0])
    child_copy = pltpu.make_async_copy(child_hbm, child_ref, sems.at[1])

    @pl.when(first | upright)
    def _():
        front_copy.start()

    @pl.when(hit | upright)
    def _():
        child_copy.start()

    @pl.when(jnp.logical_not(first))
    def _():
        acc_ref[...] = jnp.zeros_like(acc_ref)

    @pl.when(first)
    def _():
        front_copy.wait()
        for z in range(2):
            for j in range(SLOTS):
                acc_ref[j, z] = front_ref[z, pl.ds(j, BLK, stride=SLOTS), :]

    @pl.when(hit)
    def _():
        child_copy.wait()
        for k in range(CHILD_SLOTS):
            slot = map_ref[child, k * RANKS + col] // RANKS
            for z in range(2):
                acc_ref[slot, z] += child_ref[z, pl.ds(k, BLK, stride=CHILD_SLOTS), :]

    @pl.when(upright)
    def _():
        front_copy.wait()
        child_copy.wait()
        for z in range(2):
            acc_ref[leaf, z] = front_ref[z, pl.ds(0, BLK, stride=SLOTS), :].T
        for k in range(CHILD_SLOTS):
            @pl.when(map_ref[child, k * RANKS + col] < RANKS)
            def _():
                for z in range(2):
                    acc_ref[target // RANKS, z] += child_ref[z, pl.ds(k, BLK, stride=CHILD_SLOTS), :].T

    for d in range(SLOTS):
        for z in range(2):
            out_ref[d, z, :BLK, :] = acc_ref[d, z].astype(BF16)
            out_ref[d, z, BLK:, :] = acc_ref[0, z, d * SLICE : (d + 1) * SLICE, :].astype(BF16)


def top_rows(child_map, front, child):
    return pl.pallas_call(
        top_rows_kernel,
        out_shape=jax.ShapeDtypeStruct((SLOTS, 2, BLK + SLICE, BLK), BF16),
        in_specs=[smem(), hbm(), hbm()],
        out_specs=vmem(),
        scratch_shapes=[
            pltpu.VMEM((SLOTS, 2, BLK, BLK), F32),
            pltpu.VMEM(front.shape, F32),
            pltpu.VMEM(child.shape, F32),
            pltpu.SemaphoreType.DMA((2,)),
        ],
        compiler_params=params(LARGE),
        name="top_rows",
    )(child_map, front, child)


def route_kernel(map_ref, real_ref, upper_ref, lower_ref, out_ref):
    leaf, row = lax.axis_index("leaf"), lax.axis_index("row")
    child = leaf // CHILD_SLOTS
    out_ref[...] = jnp.zeros_like(out_ref)
    for k in range(CHILD_SLOTS):
        target = map_ref[child, k * RANKS + row] // RANKS
        out_ref[target, :BLK, :] = real_ref[pl.ds(k, BLK, stride=CHILD_SLOTS), :].T
        where = pl.ds(k, BLK // 2, stride=CHILD_SLOTS)
        imag = jnp.concatenate([upper_ref[where, :], lower_ref[where, :]], axis=0)
        out_ref[target, BLK : 2 * BLK, :] = imag.T
    for d in range(SLOTS):
        out_ref[d, 2 * BLK :, :] = real_ref[CHILD_SLOTS * BLK :, :]


def route(child_map, real, upper, lower):
    return pl.pallas_call(
        route_kernel,
        out_shape=jax.ShapeDtypeStruct((SLOTS, 2 * BLK + TAG, BLK), F32),
        in_specs=[smem(), vmem(), vmem(), vmem()],
        out_specs=vmem(),
        compiler_params=params(SMALL),
        cost_estimate=pl.CostEstimate(flops=1 << 20, bytes_accessed=2 << 20, transcendentals=0),
        name="route",
    )(child_map, real, upper, lower)


def assemble_kernel(map_ref, front_ref, pieces_ref, out_ref):
    col = lax.axis_index("col")
    out_ref[...] = front_ref[...]
    for child in range(2):
        for k in range(CHILD_SLOTS):
            slot = map_ref[child, k * RANKS + col] // RANKS
            where = pl.ds(slot, BLK, stride=SLOTS)
            for z in range(2):
                out_ref[z, where, :] += pieces_ref[child * CHILD_SLOTS + k, z]


def assemble(child_map, front, pieces):
    return pl.pallas_call(
        assemble_kernel,
        out_shape=jax.ShapeDtypeStruct(front.shape, F32),
        in_specs=[smem(), vmem(), vmem()],
        out_specs=vmem(),
        compiler_params=params(SMALL),
        cost_estimate=pl.CostEstimate(flops=1 << 20, bytes_accessed=3 << 20, transcendentals=0),
        name="assemble",
    )(child_map, front, pieces)


def split(x):
    high = x.astype(BF16)
    return high, (x - high.astype(F32)).astype(BF16)


def dot(a, b):
    return jnp.dot(a, b, preferred_element_type=F32)


def real_product(a, b):
    return dot(a[0], b[0]) if len(a) == 1 else dot(a[0], b[0]) + (dot(a[0], b[1]) + dot(a[1], b[0]))


def product(left, right):
    return (
        real_product(left[0], right[0]) - real_product(left[1], right[1]),
        real_product(left[0], right[1]) + real_product(left[1], right[0]),
    )


def rounded(pair):
    return [(x.astype(BF16),) for x in pair]


def multipliers_kernel(mine_ref, other_ref, half_ref, rest_ref, mult_ref, sent_ref, a_ref):
    width = 2 * BLK
    left_here = lax.axis_index("col") % 2 == 0
    for d in range(RANKS):
        for h in range(2):
            for z in range(2):
                mine = mine_ref[d, z, h * SLICE : (h + 1) * SLICE, :].astype(F32)
                other = other_ref[d, z, h * SLICE : (h + 1) * SLICE, :].astype(F32)
                where = slice(h * BLK + d * SLICE, h * BLK + (d + 1) * SLICE)
                a_ref[z, where, :BLK] = jnp.where(left_here, mine, other)
                a_ref[z, where, BLK:] = jnp.where(left_here, other, mine)
    a_re, a_im = a_ref[0], a_ref[1]
    diagonal = lax.broadcasted_iota(jnp.int32, (width, width), 0) == lax.broadcasted_iota(
        jnp.int32, (width, width), 1
    )
    d_re = jnp.sum(jnp.where(diagonal, a_re, 0.0), axis=1, keepdims=True)
    d_im = jnp.sum(jnp.where(diagonal, a_im, 0.0), axis=1, keepdims=True)
    size = d_re * d_re + d_im * d_im
    x_re, x_im = d_re / size, -d_im / size
    e_re = jnp.where(diagonal, 0.0, -(x_re * a_re - x_im * a_im))
    e_im = jnp.where(diagonal, 0.0, -(x_re * a_im + x_im * a_re))
    e0 = (e_re, e_im)
    e0_high = rounded(e0)
    e1 = rounded(product(e0_high, e0_high))
    e2 = rounded(product(e1, e1))
    r_re, r_im = (
        jnp.concatenate(
            [
                jnp.where(left_here, half_ref[z], rest_ref[z]),
                jnp.where(left_here, rest_ref[z], half_ref[z]),
            ],
            axis=0,
        ).astype(F32)
        for z in range(2)
    )
    t = (x_re * r_re - x_im * r_im, x_re * r_im + x_im * r_re)
    step = product([split(x) for x in e0], [split(x) for x in t])
    t = (t[0] + step[0], t[1] + step[1])
    for e in (e1, e2):
        step = product(e, rounded(t))
        t = (t[0] + step[0], t[1] + step[1])
    w_re, w_im = t[0].T, t[1].T
    mult_ref[0] = w_re
    mult_ref[1] = w_im
    sent_ref[0] = w_re.astype(BF16)
    sent_ref[1] = w_im.astype(BF16)


def multipliers(mine, other, half, rest):
    width = 2 * BLK
    return pl.pallas_call(
        multipliers_kernel,
        out_shape=(
            jax.ShapeDtypeStruct((2, BLK, width), F32),
            jax.ShapeDtypeStruct((2, BLK, width), BF16),
        ),
        in_specs=[vmem()] * 4,
        out_specs=(vmem(), vmem()),
        scratch_shapes=[pltpu.VMEM((2, width, width), F32)],
        compiler_params=params(SMALL),
        cost_estimate=pl.CostEstimate(flops=3 << 30, bytes_accessed=1 << 20, transcendentals=0),
        name="multipliers",
    )(mine, other, half, rest)


def update_kernel(
    w_ref, near_ref, far_ref, mult_ref, front_ref, q0_ref, q1_ref, q2_ref, q3_ref, out_ref, panel_ref
):
    leaf, row, col = (lax.axis_index(name) for name in ("leaf", "row", "col"))
    is_pivot_row = (leaf == 0) & (row < 2)

    @pl.when(is_pivot_row)
    def _():
        out_ref[...] = front_ref[...]

    @pl.when(jnp.logical_not(is_pivot_row))
    def _():
        w_re, w_im = (
            jnp.where(col < 2, w_ref[z], jnp.where(col < 4, near_ref[z], far_ref[z])) for z in range(2)
        )
        left = jnp.concatenate(
            [jnp.concatenate([w_re, -w_im], axis=1), jnp.concatenate([w_im, w_re], axis=1)], axis=0
        )
        for step, part_ref in enumerate((q0_ref, q1_ref, q2_ref, q3_ref)):
            start = ((row % QUARTERS) ^ (0, 1, 3, 2)[step]) * QUARTER
            for z in range(2):
                for h in range(2):
                    where = pl.ds(pl.multiple_of((z * 2 + h) * BLK + start, QUARTER), QUARTER)
                    panel_ref[:, where, :] = part_ref[:, z, h * QUARTER : (h + 1) * QUARTER]
        for j in range(SLOTS):
            update = dot(left, panel_ref[j])
            where = pl.ds(j, BLK, stride=SLOTS)
            for z in range(2):
                out_ref[z, where, :] = front_ref[z, where, :] - update[z * BLK : (z + 1) * BLK]
        for g in range(2):
            @pl.when(col == g)
            def _():
                for z in range(2):
                    out_ref[z, pl.ds(0, BLK, stride=SLOTS), :] = mult_ref[z, :, g * BLK : (g + 1) * BLK]


def update(w, near, far, mult, front, quarters):
    return pl.pallas_call(
        update_kernel,
        out_shape=jax.ShapeDtypeStruct(front.shape, F32),
        in_specs=[vmem()] * 9,
        out_specs=vmem(),
        scratch_shapes=[pltpu.VMEM((SLOTS, 4 * BLK, BLK), BF16)],
        compiler_params=params(SMALL),
        name="update",
    )(w, near, far, mult, front, *quarters)


def exchange(x, axis):
    return lax.all_to_all(x, axis, 0, 0)


def spread(x, axis):
    return exchange(jnp.broadcast_to(x[None], (RANKS,) + x.shape), axis)


def shrink(child):
    largest = jnp.max(jnp.abs(child))
    exponent = jnp.clip(jnp.floor(jnp.log2(largest)), -100.0, 127.0)
    values = (child * jnp.exp2(TOP - exponent)).astype(F16)
    tag = jnp.broadcast_to(exponent.astype(F16), (TAG, BLK))
    return jnp.concatenate([values[0], tag], axis=0), values[1]


def local(parent_front, child_updates, child_map):
    front = parent_front.reshape(2, BLK * SLOTS, BLK)
    child = child_updates.reshape(2, BLK * CHILD_SLOTS, BLK)
    swap = [(a * RANKS + b, b * RANKS + a) for a in range(RANKS) for b in range(RANKS)]
    real_part, imag_part = shrink(child)
    real_part = lax.ppermute(real_part, ("row", "col"), swap)
    parts = exchange(top_rows(child_map, front, child), "leaf")
    top = jnp.sum(parts.astype(F32), axis=0).astype(BF16)
    top, real_part = lax.optimization_barrier((top, real_part))
    half, pivot = top[:, :BLK], top[:, BLK:]
    parts = half.reshape(2, QUARTERS, QUARTER, BLK).transpose(1, 0, 2, 3)
    parts = jnp.concatenate(
        [
            jnp.concatenate([parts, parts], axis=0),
            jnp.broadcast_to(pivot[None], (RANKS,) + pivot.shape),
        ],
        axis=2,
    )
    both = exchange(parts, "row")
    row, col = lax.axis_index("row"), lax.axis_index("col")
    corner = lax.ppermute(half, ("row", "col"), [(1, RANKS), (RANKS, 1)])
    half = jnp.where((row < 2) & (row != col), corner, half)
    rest = lax.ppermute(half, "col", [(0, 1), (1, 0)])
    upper, lower = imag_part[: CHILD_SLOTS * BLK // 2], imag_part[CHILD_SLOTS * BLK // 2 :]
    upper = lax.ppermute(upper, ("row", "col"), swap)
    both, rest, upper = lax.optimization_barrier((both, rest, upper))
    lower = lax.ppermute(lower, ("row", "col"), swap)
    got = spread(
        jnp.concatenate(
            [both[0, :, :QUARTER], both[1, :, :QUARTER], both[0, :, QUARTER:], both[1, :, QUARTER:]],
            axis=1,
        ),
        "leaf",
    )
    routed = route(child_map, real_part.astype(F32), upper.astype(F32), lower.astype(F32)).astype(F16)
    _, routed = lax.optimization_barrier((got, routed))
    pieces = exchange(routed, "leaf")
    mine = got[:, :, 2 * QUARTER :]
    other = lax.ppermute(mine, "col", [(0, 1), (1, 0)])
    mult, w = multipliers(mine, other, half, rest)
    quarters = [got[:, :, : 2 * QUARTER]]
    for bit in (1, 3, 2):
        step = [(a, a ^ bit) for a in range(RANKS)]
        quarters.append(lax.ppermute(quarters[0], "row", step))
    near = lax.ppermute(w, "col", [(0, 2), (1, 3)])
    far = lax.ppermute(
        jnp.where(col < 2, w, near), "col", [(0, 4), (1, 5), (2, 6), (3, 7)]
    )
    scale = jnp.exp2(pieces[:, 2 * BLK, 0].astype(F32) - TOP)
    pieces = pieces[:, : 2 * BLK].astype(F32) * scale[:, None, None]
    assembled = assemble(child_map, front, pieces.reshape(SLOTS, 2, BLK, BLK))
    result = update(w, near, far, mult, assembled, quarters)
    return result.reshape(parent_front.shape)


def solution(mesh):
    spec = P(None, None, ("leaf", "row"), None, "col")
    return jax.shard_map(
        local, mesh=mesh, in_specs=(spec, spec, P()), out_specs=spec, check_vma=False
    )
```
